32 devices in a mesh: groups: 2 (over y), prefill: 16 (over z, x, core).
Axes of the slice: x: 2, y: 2, z: 4, core: 2. Of those that a mesh axis runs over, the one named last changes fastest.
Arguments:
- queries: bfloat16 [4096, 8192], P(('groups', 'prefill')), parts along dimension 0, may hold values from -200 to 200, as said below
- keys: bfloat16 [4096, 8192], P(('groups', 'prefill')), parts along dimension 0, may hold values from -6 to 6
- values: bfloat16 [4096, 8192], P(('groups', 'prefill')), parts along dimension 0, may hold values from -24 to 24
- span_prompt: int32 [32], P('groups'), parts along dimension 0, may hold values from 0 to 4, never falling along the last dimension, each value on 1 to 6 neighbouring positions
- tails: int32 [10], P('groups'), parts along dimension 0, may hold values from 1 to 128, as said below
- owners: int32 [10], P('groups'), parts along dimension 0, may hold values from 0 to 15
Outputs:
- attended: bfloat16 [4096, 8192], P(('groups', 'prefill')), parts along dimension 0
- key_cache: bfloat16 [4096, 8192], P(('groups', 'prefill')), parts along dimension 0
- value_cache: bfloat16 [4096, 8192], P(('groups', 'prefill')), parts along dimension 0
The draws below stay inside these ranges and needn't reach their ends.
There are 2 independent parts, one for each index of `groups`. The reference program is written for one: setup_inputs(seed, part) draws one part's arguments, and reference() takes and returns one part's arrays. A program takes and returns all parts, laid end to end along the dimension named above; each array names one. Nothing has to cross between parts.
Inputs may be any that keep to these rules, and one draw needn't show every extreme that they name: `queries`: queries are of order one; a few may be large. `tails`: the first prompt's last span is full. `span_prompt`: the spans of one prompt stand in a row, in order.
All inputs are finite; a program needn't handle non-finite values.
Results may differ from the reference program's by a relative error of at most 0.0032.
Values may be sent and summed in bfloat16 or wider, within the bound.
A program may use at most 128 MiB of HBM per device.

```python
import math
import jax
import jax.numpy as jnp
import numpy as np
from jax import lax

HEADS = 64
DH = 128
CH = 128
MAXC = 6
NCH = 16
PROMPTS = 5
TOKENS = 2048
N_PREFILL = 16


def drawn_rows(key):
    width = HEADS * DH
    base = jnp.clip(jax.random.normal(jax.random.fold_in(key, 11), (TOKENS, width), jnp.float32), -6.0, 6.0)
    return base


def draw_keys(key, part):
    base = drawn_rows(key)
    result = base
    return result.astype(jnp.bfloat16)


def draw_queries(key, part):
    key = jax.random.fold_in(key, 2)
    entries = 2.0 * jnp.clip(jax.random.normal(key, (TOKENS, HEADS * DH), jnp.float32), -6.0, 6.0)
    result = entries
    return result.astype(jnp.bfloat16)


def draw_tails(key, part):
    key = jax.random.fold_in(key, 3)
    drawn = jax.random.randint(key, (PROMPTS,), 1, CH + 1).astype(jnp.int32)
    return drawn.at[0].set(CH)


def plant(values, rng, low, top_value):
    dims = values.shape
    spot = [jax.random.randint(jax.random.fold_in(rng, axis), (), 0, dims[axis]) for axis in range(len(dims))]
    values = values.at[tuple(spot)].set(low)
    longest = dims.index(max(dims))
    spot[longest] = (spot[longest] + 1) % dims[longest]
    return values.at[tuple(spot)].set(top_value)


def block_scale(rng, shape, cuts, least, top_value):
    loudness = 1.0
    for dim, shards_of in cuts:
        draws = jax.random.uniform(jax.random.fold_in(jax.random.fold_in(rng, 6), dim), (shards_of,), jnp.float32, least / len(cuts), top_value / len(cuts))
        loudness = loudness * jnp.repeat(jnp.exp(draws), shape[dim] // shards_of).reshape((-1,) + (1,) * (len(shape) - 1 - dim))
    return loudness


def split_up(amount, total, limit, skew):
    portions = [(1 << 20) // math.isqrt(rank ** skew) + 1 for rank in range(2, amount + 1)]
    rest, counts = total - limit - (amount - 1), [1] * (amount - 1)
    while rest > 0:
        candidates = [i for i in range(amount - 1) if counts[i] < limit]
        whole, budget = sum([portions[i] for i in candidates]), rest
        for i in candidates:
            more = min(limit - counts[i], max(1, budget * portions[i] // whole), rest)
            counts[i] = counts[i] + more
            rest = rest - more
    return np.array([limit] + counts)


def ragged(rng, number_of, total, bound, lean):
    if number_of == 2:
        one = jax.random.randint(rng, (), max(1, total - bound), min(bound, total - 1) + 1)
        return jnp.stack([one, total - one])
    tallies = jnp.asarray(split_up(number_of, total, bound, lean), jnp.int32)
    couples = (number_of - 1) // 2
    source_of, sink = tallies[1:1 + 2 * couples:2], tallies[2:2 + 2 * couples:2]
    room = jnp.minimum(source_of - 1, bound - sink)
    shifted = jax.random.randint(jax.random.fold_in(rng, 1), (couples,), 0, 1 << 20) % (room + 1)
    tallies = tallies.at[1:1 + 2 * couples:2].set(source_of - shifted).at[2:2 + 2 * couples:2].set(sink + shifted)
    return tallies[jax.random.permutation(jax.random.fold_in(rng, 2), number_of)]


def noise(stream_key, dims, spread, most, pieces=(), held_as=jnp.bfloat16):
    gain = block_scale(stream_key, dims, pieces, -0.22, 0.18) if pieces else 1.0
    values = jax.random.normal(stream_key, dims, jnp.float32) * spread * gain
    return jnp.minimum(jnp.maximum(values, -most), most).astype(held_as)


def setup_inputs(seed: int = 0, part: int = 0) -> dict:
    splits = jax.random.split(jax.random.key(seed), 7)
    part_splits = jax.random.split(jax.random.fold_in(splits[6], part), 7)
    queries = draw_queries(jax.random.fold_in(jax.random.fold_in(splits[6], part), 71), part)
    keys = draw_keys(jax.random.fold_in(jax.random.fold_in(splits[6], part), 71), part)
    values = noise(part_splits[2], (TOKENS, HEADS * DH), 4.0, 24.0, ((0, 16),))
    span_prompt = jnp.searchsorted(jnp.cumsum(ragged(part_splits[3], PROMPTS, NCH, MAXC, 2)), jnp.arange(NCH), side="right").astype(jnp.int32)
    tails = draw_tails(jax.random.fold_in(jax.random.fold_in(splits[6], part), 71), part)
    owners = plant(jax.random.randint(part_splits[5], (PROMPTS,), 0, N_PREFILL), jax.random.fold_in(part_splits[5], 1), 0, N_PREFILL - 1).astype(jnp.int32)
    return {"queries": queries, "keys": keys, "values": values, "span_prompt": span_prompt, "tails": tails, "owners": owners}


def span_layout(span_prompt, tails):
    count_all = span_prompt.shape[0]
    index = jnp.arange(count_all, dtype=jnp.int32)
    same = span_prompt[:, None] == span_prompt[None, :]
    order = jnp.sum(same & (index[None, :] < index[:, None]), axis=1).astype(jnp.int32)
    count = jnp.sum(same, axis=1).astype(jnp.int32)
    length = (count - 1) * CH + tails[span_prompt]
    return order, length.astype(jnp.int32)


def reference(queries, keys, values, span_prompt, tails, owners):
    width = HEADS * DH
    devices = N_PREFILL
    order, length = span_layout(span_prompt, tails)
    lead = jnp.zeros(((MAXC - 1) * CH, width), jnp.bfloat16)
    padded_keys = jnp.concatenate([lead, keys], axis=0)
    padded_values = jnp.concatenate([lead, values], axis=0)
    scale = 1.0 / (DH ** 0.5)
    rows = jnp.arange(CH, dtype=jnp.int32)
    window = jnp.arange(MAXC * CH, dtype=jnp.int32)

    def one_span(span):
        start = (span * CH).astype(jnp.int32)
        query_block = lax.dynamic_slice(queries, (start, jnp.int32(0)), (CH, width))
        key_block = lax.dynamic_slice(padded_keys, (start, jnp.int32(0)), (MAXC * CH, width))
        value_block = lax.dynamic_slice(padded_values, (start, jnp.int32(0)), (MAXC * CH, width))
        key_span = span - (MAXC - 1) + window // CH
        clipped = jnp.maximum(key_span, 0)
        key_pos = order[clipped] * CH + window % CH
        query_pos = order[span] * CH + rows
        allowed = (key_span[None, :] >= 0) & (span_prompt[clipped][None, :] == span_prompt[span])
        allowed = allowed & (key_pos[None, :] <= query_pos[:, None]) & (key_pos[None, :] < length[span])
        q3 = query_block.reshape(CH, HEADS, DH).astype(jnp.float32)
        k3 = key_block.reshape(MAXC * CH, HEADS, DH).astype(jnp.float32)
        v3 = value_block.reshape(MAXC * CH, HEADS, DH).astype(jnp.float32)
        score = jnp.einsum('qhd,khd->hqk', q3, k3) * scale
        masked = jnp.where(allowed[None], score, -jnp.inf)
        top = jnp.max(masked, axis=-1, keepdims=True)
        weight = jnp.where(allowed[None], jnp.exp(score - top), jnp.float32(0.0))
        total = jnp.sum(weight, axis=-1)
        rounded = lax.optimization_barrier(weight.astype(jnp.bfloat16)).astype(jnp.float32)
        mixed = jnp.einsum('hqk,khd->qhd', rounded, v3) / jnp.transpose(total)[:, :, None]
        used = (query_pos < length[span])[:, None, None]
        mixed = jnp.where(used, mixed, jnp.float32(0.0))
        return mixed.reshape(CH, width).astype(jnp.bfloat16)

    attended = lax.map(one_span, jnp.arange(devices, dtype=jnp.int32)).reshape(CH * devices, width)
    slot = jnp.arange(CH * devices, dtype=jnp.int32)
    slot_pos = order[slot // CH] * CH + slot % CH
    slot_used = (slot_pos < length[slot // CH])[:, None]
    masked_keys = jnp.where(slot_used, keys, jnp.zeros_like(keys))
    masked_values = jnp.where(slot_used, values, jnp.zeros_like(values))
    target = slot // CH
    within = (slot % CH) // devices
    source = slot % devices
    owner = owners[span_prompt[source]]
    picked = source * CH + (target - owner) % devices + within * devices
    return attended, jnp.take(masked_keys, picked, axis=0), jnp.take(masked_values, picked, axis=0)
```

```python
import functools
import jax
import jax.numpy as jnp
from jax import lax
from jax.experimental import pallas as pl
from jax.experimental.pallas import tpu as pltpu
from jax.sharding import PartitionSpec as P

HEADS = 64
MAXC = 6
CHUNKS = 4
SLOTS = 5
MESH = pl.DeviceIdType.MESH


def from_behind(array, axis, by):
    devices = lax.axis_size(axis)
    pairs = [(i, i + by) for i in range(devices) if 0 <= i + by < devices]
    return lax.ppermute(array, axis, pairs)


def pick_entry(table, where_at):
    index = jnp.arange(table.shape[0], dtype=jnp.int32)
    return jnp.sum(jnp.where(index == where_at, table, 0))


def local(queries, keys, values, span_prompt, tails, owners):
    rows, width = queries.shape
    depth = width // HEADS
    count_dev = lax.axis_size("prefill")
    me_index = lax.axis_index("prefill")
    span_index = jnp.arange(span_prompt.shape[0], dtype=jnp.int32)
    prompt_id = pick_entry(span_prompt, me_index)
    mine = span_prompt == prompt_id
    order = jnp.sum(mine & (span_index < me_index))
    count = jnp.sum(mine)
    length = (count - 1) * rows + pick_entry(tails, prompt_id)
    owner = pick_entry(owners, prompt_id)
    local_rows = jnp.arange(rows, dtype=jnp.int32)
    query_pos = order * rows + local_rows
    used = query_pos < length
    blocks = [(keys, values)]
    carried = (keys, values)
    for step in range(1, MAXC):
        carried = from_behind((carried[0], carried[1]), "prefill", 1)
        blocks.append(carried)
    scale = 1.0 / depth**0.5
    query_heads = queries.reshape(rows, HEADS, depth)
    own_allowed = (local_rows[None, :] <= local_rows[:, None]) & (
        (order * rows + local_rows)[None, :] < length
    )
    scores = []
    allowed_list = []
    for step in range(MAXC):
        key_heads = blocks[step][0].reshape(rows, HEADS, depth)
        score = (
            jnp.einsum("qhd,khd->hqk", query_heads, key_heads, preferred_element_type=jnp.float32)
            * scale
        )
        if step == 0:
            allowed = own_allowed[None]
        else:
            allowed = jnp.broadcast_to(step <= order, (1, 1, 1))
        scores.append(score)
        allowed_list.append(allowed)
    top = jnp.full((HEADS, rows, 1), -jnp.inf, jnp.float32)
    for step in range(MAXC):
        masked = jnp.where(allowed_list[step], scores[step], -jnp.inf)
        top = jnp.maximum(top, jnp.max(masked, axis=-1, keepdims=True))
    total = jnp.zeros((HEADS, rows), jnp.float32)
    mixed = jnp.zeros((rows, HEADS, depth), jnp.float32)
    for step in range(MAXC):
        weight = jnp.where(allowed_list[step], jnp.exp(scores[step] - top), jnp.float32(0.0))
        total = total + jnp.sum(weight, axis=-1)
        value_heads = blocks[step][1].reshape(rows, HEADS, depth)
        mixed = mixed + jnp.einsum(
            "hqk,khd->qhd",
            weight.astype(jnp.bfloat16),
            value_heads,
            preferred_element_type=jnp.float32,
        )
    mixed = mixed / jnp.transpose(total)[:, :, None]
    mixed = jnp.where(used[:, None, None], mixed, jnp.float32(0.0))
    attended = mixed.reshape(rows, width).astype(jnp.bfloat16)
    masked_keys = jnp.where(used[:, None], keys, jnp.zeros_like(keys))
    masked_values = jnp.where(used[:, None], values, jnp.zeros_like(values))
    rolled_keys = jnp.roll(masked_keys.reshape(rows // count_dev, count_dev, width), owner, axis=1)
    rolled_values = jnp.roll(
        masked_values.reshape(rows // count_dev, count_dev, width), owner, axis=1
    )
    got_keys, got_values = (
        lax.all_to_all(rolled_keys, "prefill", split_axis=1, concat_axis=1, tiled=True),
        lax.all_to_all(rolled_values, "prefill", split_axis=1, concat_axis=1, tiled=True),
    )
    return (attended, got_keys.reshape(rows, width), got_values.reshape(rows, width))


def exchange_kernel(
    sp, tails, owners, q_ref, k_ref, v_ref, att_ref, got_ref,
    packed, slots, recv, send_a, send_b, recv_r, send_r, send_f, send_x, local_sem,
):
    rows, width = q_ref.shape
    depth = width // HEADS
    cw = width // CHUNKS
    me = lax.axis_index("prefill")
    z, x, c = me // 4, (me // 2) % 2, me % 2
    sibling = me + 1 - 2 * c
    others = [lax.rem(me + k, 16) for k in range(1, 16)]

    prompt = sp[me]
    order = jnp.int32(0)
    count = jnp.int32(0)
    for j in range(16):
        same = jnp.where(sp[j] == prompt, 1, 0)
        count = count + same
        order = order + jnp.where(j < me, same, 0)
    used_rows = (count - 1 - order) * rows + tails[prompt]
    owner = owners[prompt]
    spans = [
        4 * z - 4 * (1 - x),
        4 * z - 4 * (1 - x) + 1,
        4 * z - 2,
        4 * z - 1,
        jnp.where(c == 1, me - 1, me - 5),
    ]
    flags = [
        jnp.where(s >= 0, jnp.where(sp[jnp.maximum(s, 0)] == prompt, 1, 0), 0) for s in spans
    ]

    def clear(slot):
        @pl.loop(0, 2 * width // 512)
        def _(n):
            slots[slot, :, pl.ds(pl.multiple_of(n * 512, 512), 512)] = jnp.zeros(
                (rows, 512), jnp.bfloat16
            )

    for s in range(SLOTS):
        pl.when(spans[s] < 0)(functools.partial(clear, s))

    barrier = pltpu.get_barrier_semaphore()
    for other in others:
        pl.semaphore_signal(barrier, inc=1, device_id={"prefill": other}, device_id_type=MESH)
    pl.semaphore_wait(barrier, 15)

    def remote(src, dst, ssem, rsem, to):
        return pltpu.make_async_remote_copy(
            src_ref=src, dst_ref=dst, send_sem=ssem, recv_sem=rsem,
            device_id={"prefill": to}, device_id_type=MESH,
        )

    started = []

    def go(cond, copy):
        pl.when(cond)(copy.start)
        started.append((cond, copy))

    def cols(ch):
        return pl.ds(ch * 2 * cw, 2 * cw)

    zslot = 2 * x + c

    r = lax.broadcasted_iota(jnp.int32, (rows, rows), 0)
    t = lax.broadcasted_iota(jnp.int32, (rows, rows), 1)
    wanted = (((r >> 3) - owner) & 15) + ((r & 7) << 4)
    moves = jnp.where((t == wanted) & (t < used_rows), 1.0, 0.0).astype(jnp.bfloat16)
    for ch in range(CHUNKS):
        for part, ref in ((0, k_ref), (1, v_ref)):
            @pl.loop(0, cw // 256)
            def _(n, ch=ch, part=part, ref=ref):
                at = pl.multiple_of(n * 256, 256)
                block = ref[:, pl.ds(ch * cw + at, 256)]
                packed[:, pl.ds((2 * ch + part) * cw + at, 256)] = jnp.dot(
                    moves, block, preferred_element_type=jnp.float32
                ).astype(jnp.bfloat16)

        own = packed.at[:, cols(ch)]
        go(z < 3, remote(own, slots.at[zslot, :, cols(ch)], send_a.at[0, ch],
                         recv.at[zslot, ch], lax.rem(me + 4, 16)))
        go(x == 0, remote(own, slots.at[c, :, cols(ch)], send_a.at[1, ch],
                          recv.at[c, ch], lax.rem(me + 2, 16)))
        go(c == 0, remote(own, slots.at[4, :, cols(ch)], send_a.at[2, ch],
                          recv.at[4, ch], sibling))

    def block(ref, chip):
        return ref.at[pl.ds(pl.multiple_of(chip * 16, 16), 16), :]

    my_chip = me // 2
    keep = pltpu.make_async_copy(block(packed, my_chip), got_ref.at[me], local_sem.at[4])
    keep.start()
    go(me >= 0, remote(block(packed, my_chip), got_ref.at[me], send_r.at[7], recv_r.at[me], sibling))
    go(x == 1, remote(block(packed, lax.rem(my_chip + 7, 8)), got_ref.at[me], send_r.at[6],
                      recv_r.at[me], lax.rem(me + 14, 16)))
    for zp in (2, 1, 0):
        for xp in range(2):
            go(zp < z, remote(block(packed, 2 * zp + xp), got_ref.at[me], send_r.at[2 * zp + xp],
                              recv_r.at[me], lax.rem(4 * zp + 2 * xp + c, 16)))

    def arrived(slot, ch):
        ref = slots.at[slot, :, cols(ch)]
        pltpu.make_async_copy(ref, ref, recv.at[slot, ch]).wait()

    def relay(ch):
        @pl.when(z >= 1)
        def _():
            arrived(zslot, ch)
        here = slots.at[zslot, :, cols(ch)]
        go((z >= 1) & (x == 1), remote(here, slots.at[2 + c, :, cols(ch)], send_b.at[0, ch],
                                       recv.at[2 + c, ch], lax.rem(me + 14, 16)))
        go((z >= 1) & (x == 0) & (c == 1), remote(here, slots.at[4, :, cols(ch)], send_b.at[1, ch],
                                                  recv.at[4, ch], lax.rem(me + 1, 16)))
        go(z >= 1, remote(here, slots.at[zslot, :, cols(ch)], send_b.at[2, ch],
                          recv.at[zslot, ch], sibling))
        second = 2 * (1 - x) + c
        has = (x == 1) | (z >= 1)

        @pl.when(has)
        def _():
            arrived(second, ch)
        there = slots.at[second, :, cols(ch)]
        go((x == 0) & (z >= 1) & (z < 3) & (c == 1),
           remote(there, slots.at[4, :, cols(ch)], send_b.at[3, ch], recv.at[4, ch],
                  lax.rem(me + 3, 16)))
        go(has, remote(there, slots.at[second, :, cols(ch)], send_b.at[4, ch],
                       recv.at[second, ch], sibling))

    scale = 1.0 / depth**0.5
    causal = (t <= r) & (t < used_rows)
    keep_row = lax.broadcasted_iota(jnp.int32, (rows, depth), 0) < used_rows
    masks = [jnp.full((rows, rows), f, jnp.int32) > 0 for f in flags]

    def attention(ch):
        @pl.when(z >= 1)
        def _():
            arrived(2 * x + (1 - c), ch)

        @pl.when((x == 1) | (z >= 1))
        def _():
            arrived(2 * (1 - x) + (1 - c), ch)

        @pl.when(spans[4] >= 0)
        def _():
            arrived(4, ch)

        @pl.loop(0, HEADS // CHUNKS)
        def _(n):
            at = pl.multiple_of(n * depth, depth)
            mine = pl.ds(ch * cw + at, depth)
            kcols = pl.ds(2 * ch * cw + at, depth)
            vcols = pl.ds((2 * ch + 1) * cw + at, depth)
            q = q_ref[:, mine]
            dims = (((1,), (1,)), ((), ()))
            scores = [
                jnp.where(causal, lax.dot_general(
                    q, k_ref[:, mine], dims, preferred_element_type=jnp.float32) * scale, -jnp.inf)
            ]
            for s in range(SLOTS):
                score = lax.dot_general(
                    q, slots[s, :, kcols], dims, preferred_element_type=jnp.float32) * scale
                scores.append(jnp.where(masks[s], score, -jnp.inf))
            top = functools.reduce(jnp.maximum, scores)
            top = jnp.max(top, axis=1, keepdims=True)
            weights = [jnp.exp(s - top) for s in scores]
            total = jnp.sum(functools.reduce(jnp.add, weights), axis=1, keepdims=True)
            mixed = jnp.dot(weights[0].astype(jnp.bfloat16), v_ref[:, mine],
                            preferred_element_type=jnp.float32)
            for s in range(SLOTS):
                mixed = mixed + jnp.dot(weights[s + 1].astype(jnp.bfloat16), slots[s, :, vcols],
                                        preferred_element_type=jnp.float32)
            mixed = jnp.where(keep_row, mixed / total, 0.0)
            att_ref[:, mine] = mixed.astype(jnp.bfloat16)

    for ch in range(CHUNKS):
        relay(ch)
        if ch == CHUNKS - 1:
            origin = lax.rem(me + 12, 16)
            rows_of = slots.at[zslot]
            go((z >= 1) & (x == 0), remote(block(rows_of, lax.rem(my_chip + 1, 8)), got_ref.at[origin],
                                           send_f.at[0], recv_r.at[origin], lax.rem(me + 2, 16)))
            for zp in (3, 2):
                for xp in range(2):
                    go((z >= 1) & (zp > z), remote(
                        block(rows_of, 2 * zp + xp), got_ref.at[origin],
                        send_f.at[1 + 2 * (zp - 2) + xp], recv_r.at[origin],
                        lax.rem(4 * zp + 2 * xp + c, 16)))
        if ch >= 1:
            attention(ch - 1)
    attention(CHUNKS - 1)

    taken = []
    for s in range(4):
        copy = pltpu.make_async_copy(
            block(slots.at[s], my_chip), got_ref.at[jnp.maximum(spans[s], 0)], local_sem.at[s])
        pl.when(spans[s] >= 0)(copy.start)
        taken.append((spans[s] >= 0, copy))

    def landed(source):
        ref = got_ref.at[source]
        pltpu.make_async_copy(ref, ref, recv_r.at[source]).wait()

    direct = []
    for zs in (3, 2, 1, 0):
        for xs in range(2):
            cond = (zs > z) | (zs < z - 1)
            if xs == 1:
                cond = cond | ((zs == z) & (x == 0))
            else:
                cond = cond | ((zs == z - 1) & (x == 1))
            direct.append((zs, xs, cond))
    for zs, xs, cond in direct:
        source = 4 * zs + 2 * xs + c

        @pl.when(cond)
        def _(source=source):
            landed(source)
        go(cond, remote(got_ref.at[source], got_ref.at[source], send_x.at[2 * zs + xs],
                        recv_r.at[source], sibling))
    landed(sibling)
    for zs, xs, cond in direct:
        source = 4 * zs + 2 * xs + 1 - c

        @pl.when(cond)
        def _(source=source):
            landed(source)

    keep.wait()
    for cond, copy in taken:
        pl.when(cond)(copy.wait)
    for cond, copy in started:
        pl.when(cond)(copy.wait_send)


def unpack_kernel(got_ref, att_in, att_out, key_out, value_out):
    core = lax.axis_index("prefill") % 2
    cw = key_out.shape[1]
    r = lax.broadcasted_iota(jnp.int32, (128, 256), 0)
    t = lax.broadcasted_iota(jnp.int32, (128, 256), 1)
    moves = jnp.where(t == ((r & 15) << 4) + core * 8 + (r >> 4), 1.0, 0.0).astype(jnp.bfloat16)
    for out, base in ((key_out, 0), (value_out, cw)):
        for n in range(cw // 512):
            out[:, n * 512:(n + 1) * 512] = jnp.dot(
                moves, got_ref[:, base + n * 512:base + (n + 1) * 512],
                preferred_element_type=jnp.float32,
            ).astype(jnp.bfloat16)
    att_out[...] = att_in[...]


def planned(queries, keys, values, span_prompt, tails, owners):
    rows, width = queries.shape
    vmem = pl.BlockSpec(memory_space=pltpu.VMEM)
    smem = pl.BlockSpec(memory_space=pltpu.SMEM)
    dma = pltpu.SemaphoreType.DMA
    attended, got = pl.pallas_call(
        exchange_kernel,
        out_shape=(
            jax.ShapeDtypeStruct((rows, width), jnp.bfloat16),
            jax.ShapeDtypeStruct((16, 16, 2 * width), jnp.bfloat16),
        ),
        in_specs=[smem] * 3 + [vmem] * 3,
        out_specs=(vmem, pl.BlockSpec(memory_space=pl.ANY)),
        scratch_shapes=[
            pltpu.VMEM((rows, 2 * width), jnp.bfloat16),
            pltpu.VMEM((SLOTS, rows, 2 * width), jnp.bfloat16),
            dma((SLOTS, CHUNKS)),
            dma((3, CHUNKS)),
            dma((5, CHUNKS)),
            dma((16,)),
            dma((8,)),
            dma((5,)),
            dma((8,)),
            dma((5,)),
        ],
        compiler_params=pltpu.CompilerParams(
            collective_id=0, has_side_effects=True, vmem_limit_bytes=52 * 2**20
        ),
        cost_estimate=pl.CostEstimate(
            flops=24 * rows * rows * width, bytes_accessed=32 * rows * width,
            transcendentals=MAXC * HEADS * rows * rows,
        ),
    )(span_prompt, tails, owners, queries, keys, values)
    cw = width // CHUNKS
    return pl.pallas_call(
        unpack_kernel,
        grid=(CHUNKS,),
        out_shape=(jax.ShapeDtypeStruct((rows, width), jnp.bfloat16),) * 3,
        in_specs=[
            pl.BlockSpec((256, 2 * cw), lambda n: (0, n)),
            pl.BlockSpec((rows, cw), lambda n: (0, n)),
        ],
        out_specs=(pl.BlockSpec((rows, cw), lambda n: (0, n)),) * 3,
        compiler_params=pltpu.CompilerParams(vmem_limit_bytes=32 * 2**20),
    )(got.reshape(256, 2 * width), attended)


def solution(mesh):
    placed = (
        P(("groups", "prefill"), None),
        P(("groups", "prefill"), None),
        P(("groups", "prefill"), None),
        P("groups"),
        P("groups"),
        P("groups"),
    )
    return jax.shard_map(
        planned if mesh.shape["prefill"] == 16 else local,
        mesh=mesh,
        in_specs=placed,
        out_specs=(
            P(("groups", "prefill"), None),
            P(("groups", "prefill"), None),
            P(("groups", "prefill"), None),
        ),
        check_vma=False,
    )
```

```python
import functools
import jax
import jax.numpy as jnp
from jax import lax
from jax.experimental import pallas as pl
from jax.experimental.pallas import tpu as pltpu
from jax.sharding import PartitionSpec as P

HEADS = 64
MAXC = 6
CHUNKS = 4
SLOTS = 5
MESH = pl.DeviceIdType.MESH


def from_behind(array, axis, by):
    devices = lax.axis_size(axis)
    pairs = [(i, i + by) for i in range(devices) if 0 <= i + by < devices]
    return lax.ppermute(array, axis, pairs)


def pick_entry(table, where_at):
    index = jnp.arange(table.shape[0], dtype=jnp.int32)
    return jnp.sum(jnp.where(index == where_at, table, 0))


def local(queries, keys, values, span_prompt, tails, owners):
    rows, width = queries.shape
    depth = width // HEADS
    count_dev = lax.axis_size("prefill")
    me_index = lax.axis_index("prefill")
    span_index = jnp.arange(span_prompt.shape[0], dtype=jnp.int32)
    prompt_id = pick_entry(span_prompt, me_index)
    mine = span_prompt == prompt_id
    order = jnp.sum(mine & (span_index < me_index))
    count = jnp.sum(mine)
    length = (count - 1) * rows + pick_entry(tails, prompt_id)
    owner = pick_entry(owners, prompt_id)
    local_rows = jnp.arange(rows, dtype=jnp.int32)
    query_pos = order * rows + local_rows
    used = query_pos < length
    blocks = [(keys, values)]
    carried = (keys, values)
    for step in range(1, MAXC):
        carried = from_behind((carried[0], carried[1]), "prefill", 1)
        blocks.append(carried)
    scale = 1.0 / depth**0.5
    query_heads = queries.reshape(rows, HEADS, depth)
    own_allowed = (local_rows[None, :] <= local_rows[:, None]) & (
        (order * rows + local_rows)[None, :] < length
    )
    scores = []
    allowed_list = []
    for step in range(MAXC):
        key_heads = blocks[step][0].reshape(rows, HEADS, depth)
        score = (
            jnp.einsum("qhd,khd->hqk", query_heads, key_heads, preferred_element_type=jnp.float32)
            * scale
        )
        if step == 0:
            allowed = own_allowed[None]
        else:
            allowed = jnp.broadcast_to(step <= order, (1, 1, 1))
        scores.append(score)
        allowed_list.append(allowed)
    top = jnp.full((HEADS, rows, 1), -jnp.inf, jnp.float32)
    for step in range(MAXC):
        masked = jnp.where(allowed_list[step], scores[step], -jnp.inf)
        top = jnp.maximum(top, jnp.max(masked, axis=-1, keepdims=True))
    total = jnp.zeros((HEADS, rows), jnp.float32)
    mixed = jnp.zeros((rows, HEADS, depth), jnp.float32)
    for step in range(MAXC):
        weight = jnp.where(allowed_list[step], jnp.exp(scores[step] - top), jnp.float32(0.0))
        total = total + jnp.sum(weight, axis=-1)
        value_heads = blocks[step][1].reshape(rows, HEADS, depth)
        mixed = mixed + jnp.einsum(
            "hqk,khd->qhd",
            weight.astype(jnp.bfloat16),
            value_heads,
            preferred_element_type=jnp.float32,
        )
    mixed = mixed / jnp.transpose(total)[:, :, None]
    mixed = jnp.where(used[:, None, None], mixed, jnp.float32(0.0))
    attended = mixed.reshape(rows, width).astype(jnp.bfloat16)
    masked_keys = jnp.where(used[:, None], keys, jnp.zeros_like(keys))
    masked_values = jnp.where(used[:, None], values, jnp.zeros_like(values))
    rolled_keys = jnp.roll(masked_keys.reshape(rows // count_dev, count_dev, width), owner, axis=1)
    rolled_values = jnp.roll(
        masked_values.reshape(rows // count_dev, count_dev, width), owner, axis=1
    )
    got_keys, got_values = (
        lax.all_to_all(rolled_keys, "prefill", split_axis=1, concat_axis=1, tiled=True),
        lax.all_to_all(rolled_values, "prefill", split_axis=1, concat_axis=1, tiled=True),
    )
    return (attended, got_keys.reshape(rows, width), got_values.reshape(rows, width))


def exchange_kernel(
    sp, tails, owners, q_ref, k_ref, v_ref, att_ref, got_ref,
    packed, slots, recv, send_a, send_b, recv_r, send_r, send_f, send_g, send_x, local_sem,
):
    rows, width = q_ref.shape
    depth = width // HEADS
    cw = width // CHUNKS
    me = lax.axis_index("prefill")
    z, x, c = me // 4, (me // 2) % 2, me % 2
    sibling = me + 1 - 2 * c
    others = [lax.rem(me + k, 16) for k in range(1, 16)]

    prompt = sp[me]
    order = jnp.int32(0)
    count = jnp.int32(0)
    for j in range(16):
        same = jnp.where(sp[j] == prompt, 1, 0)
        count = count + same
        order = order + jnp.where(j < me, same, 0)
    used_rows = (count - 1 - order) * rows + tails[prompt]
    owner = owners[prompt]
    spans = [
        4 * z - 4 * (1 - x),
        4 * z - 4 * (1 - x) + 1,
        4 * z - 2,
        4 * z - 1,
        jnp.where(c == 1, me - 1, me - 5),
    ]
    flags = [
        jnp.where(s >= 0, jnp.where(sp[jnp.maximum(s, 0)] == prompt, 1, 0), 0) for s in spans
    ]

    def clear(slot):
        @pl.loop(0, 2 * width // 512)
        def _(n):
            slots[slot, :, pl.ds(pl.multiple_of(n * 512, 512), 512)] = jnp.zeros(
                (rows, 512), jnp.bfloat16
            )

    for s in range(SLOTS):
        pl.when(spans[s] < 0)(functools.partial(clear, s))

    barrier = pltpu.get_barrier_semaphore()
    for other in others:
        pl.semaphore_signal(barrier, inc=1, device_id={"prefill": other}, device_id_type=MESH)
    pl.semaphore_wait(barrier, 15)

    def remote(src, dst, ssem, rsem, to):
        return pltpu.make_async_remote_copy(
            src_ref=src, dst_ref=dst, send_sem=ssem, recv_sem=rsem,
            device_id={"prefill": to}, device_id_type=MESH,
        )

    started = []

    def go(cond, copy):
        pl.when(cond)(copy.start)
        started.append((cond, copy))

    def cols(ch):
        return pl.ds(ch * 2 * cw, 2 * cw)

    zslot = 2 * x + c

    r = lax.broadcasted_iota(jnp.int32, (rows, rows), 0)
    t = lax.broadcasted_iota(jnp.int32, (rows, rows), 1)
    wanted = (((r >> 3) - owner) & 15) + ((r & 7) << 4)
    moves = jnp.where((t == wanted) & (t < used_rows), 1.0, 0.0).astype(jnp.bfloat16)
    for ch in range(CHUNKS):
        for part, ref in ((0, k_ref), (1, v_ref)):
            @pl.loop(0, cw // 256)
            def _(n, ch=ch, part=part, ref=ref):
                at = pl.multiple_of(n * 256, 256)
                block = ref[:, pl.ds(ch * cw + at, 256)]
                packed[:, pl.ds((2 * ch + part) * cw + at, 256)] = jnp.dot(
                    moves, block, preferred_element_type=jnp.float32
                ).astype(jnp.bfloat16)

        own = packed.at[:, cols(ch)]
        go(z < 3, remote(own, slots.at[zslot, :, cols(ch)], send_a.at[0, ch],
                         recv.at[zslot, ch], lax.rem(me + 4, 16)))
        go(x == 0, remote(own, slots.at[c, :, cols(ch)], send_a.at[1, ch],
                          recv.at[c, ch], lax.rem(me + 2, 16)))
        go(c == 0, remote(own, slots.at[4, :, cols(ch)], send_a.at[2, ch],
                          recv.at[4, ch], sibling))

    def block(ref, chip):
        return ref.at[pl.ds(pl.multiple_of(chip * 16, 16), 16), :]

    my_chip = me // 2
    keep = pltpu.make_async_copy(block(packed, my_chip), got_ref.at[me], local_sem.at[4])
    keep.start()
    go(me >= 0, remote(block(packed, my_chip), got_ref.at[me], send_r.at[7], recv_r.at[me], sibling))
    go(x == 1, remote(block(packed, lax.rem(my_chip + 7, 8)), got_ref.at[me], send_r.at[6],
                      recv_r.at[me], lax.rem(me + 14, 16)))
    for zp in (2, 1, 0):
        for xp in range(2):
            go(zp < z, remote(block(packed, 2 * zp + xp), got_ref.at[me], send_r.at[2 * zp + xp],
                              recv_r.at[me], lax.rem(4 * zp + 2 * xp + c, 16)))

    def arrived(slot, ch):
        ref = slots.at[slot, :, cols(ch)]
        pltpu.make_async_copy(ref, ref, recv.at[slot, ch]).wait()

    def relay(ch):
        @pl.when(z >= 1)
        def _():
            arrived(zslot, ch)
        here = slots.at[zslot, :, cols(ch)]
        go((z >= 1) & (x == 1), remote(here, slots.at[2 + c, :, cols(ch)], send_b.at[0, ch],
                                       recv.at[2 + c, ch], lax.rem(me + 14, 16)))
        go((z >= 1) & (x == 0) & (c == 1), remote(here, slots.at[4, :, cols(ch)], send_b.at[1, ch],
                                                  recv.at[4, ch], lax.rem(me + 1, 16)))
        go(z >= 1, remote(here, slots.at[zslot, :, cols(ch)], send_b.at[2, ch],
                          recv.at[zslot, ch], sibling))
        second = 2 * (1 - x) + c
        has = (x == 1) | (z >= 1)

        @pl.when(has)
        def _():
            arrived(second, ch)
        there = slots.at[second, :, cols(ch)]
        if ch < CHUNKS - 1:
            go((x == 0) & (z >= 1) & (z < 3) & (c == 1),
               remote(there, slots.at[4, :, cols(ch)], send_b.at[3, ch], recv.at[4, ch],
                      lax.rem(me + 3, 16)))
        else:
            go((x == 1) & (z >= 1) & (z < 3) & (c == 1),
               remote(here, slots.at[4, :, cols(ch)], send_b.at[3, ch], recv.at[4, ch],
                      lax.rem(me + 1, 16)))
        go(has, remote(there, slots.at[second, :, cols(ch)], send_b.at[4, ch],
                       recv.at[second, ch], sibling))

    scale = 1.0 / depth**0.5
    causal = (t <= r) & (t < used_rows)
    keep_row = lax.broadcasted_iota(jnp.int32, (rows, depth), 0) < used_rows
    masks = [jnp.full((rows, rows), f, jnp.int32) > 0 for f in flags]

    def attention(ch):
        @pl.when(z >= 1)
        def _():
            arrived(2 * x + (1 - c), ch)

        @pl.when((x == 1) | (z >= 1))
        def _():
            arrived(2 * (1 - x) + (1 - c), ch)

        if ch < CHUNKS - 1:
            @pl.when(spans[4] >= 0)
            def _():
                arrived(4, ch)

        @pl.loop(0, HEADS // CHUNKS)
        def _(n):
            at = pl.multiple_of(n * depth, depth)
            mine = pl.ds(ch * cw + at, depth)
            kcols = pl.ds(2 * ch * cw + at, depth)
            vcols = pl.ds((2 * ch + 1) * cw + at, depth)
            q = q_ref[:, mine]
            dims = (((1,), (1,)), ((), ()))
            scores = [
                jnp.where(causal, lax.dot_general(
                    q, k_ref[:, mine], dims, preferred_element_type=jnp.float32) * scale, -jnp.inf)
            ]
            for s in range(SLOTS):
                score = lax.dot_general(
                    q, slots[s, :, kcols], dims, preferred_element_type=jnp.float32) * scale
                scores.append(jnp.where(masks[s], score, -jnp.inf))
            top = functools.reduce(jnp.maximum, scores)
            top = jnp.max(top, axis=1, keepdims=True)
            weights = [jnp.exp(s - top) for s in scores]
            total = jnp.sum(functools.reduce(jnp.add, weights), axis=1, keepdims=True)
            mixed = jnp.dot(weights[0].astype(jnp.bfloat16), v_ref[:, mine],
                            preferred_element_type=jnp.float32)
            for s in range(SLOTS):
                mixed = mixed + jnp.dot(weights[s + 1].astype(jnp.bfloat16), slots[s, :, vcols],
                                        preferred_element_type=jnp.float32)
            mixed = jnp.where(keep_row, mixed / total, 0.0)
            att_ref[:, mine] = mixed.astype(jnp.bfloat16)

    for ch in range(CHUNKS):
        relay(ch)
        if ch == CHUNKS - 1:
            origin = lax.rem(me + 12, 16)
            rows_of = slots.at[zslot]
            go((z >= 1) & (x == 0) & (c == 0), remote(
                block(rows_of, lax.rem(my_chip + 1, 8)), got_ref.at[origin],
                send_f.at[0], recv_r.at[origin], lax.rem(me + 2, 16)))
            for zp in (3, 2):
                for xp in range(2):
                    go((z >= 1) & (zp > z) & (c == 0), remote(
                        block(rows_of, 2 * zp + xp), got_ref.at[origin],
                        send_f.at[1 + 2 * (zp - 2) + xp], recv_r.at[origin],
                        4 * zp + 2 * xp + c))
        if ch >= 1:
            attention(ch - 1)

    @pl.when(spans[4] >= 0)
    def _():
        arrived(4, CHUNKS - 1)
    fifth = jnp.maximum(spans[4], 0)
    has_fifth = (c == 0) & (spans[4] >= 0)
    for zp in (3, 2):
        for xp in range(2):
            go(has_fifth & (zp > z), remote(
                block(slots.at[4], 2 * zp + xp), got_ref.at[fifth],
                send_g.at[2 * (zp - 2) + xp], recv_r.at[fifth],
                4 * zp + 2 * xp + 1 - c))
    go(has_fifth & (x == 0), remote(
        block(slots.at[4], lax.rem(my_chip + 1, 8)), got_ref.at[fifth],
        send_g.at[4], recv_r.at[fifth], lax.rem(me + 3, 16)))
    go(has_fifth, remote(block(slots.at[4], my_chip), got_ref.at[fifth], send_g.at[5],
                         recv_r.at[fifth], sibling))
    own_fifth = pltpu.make_async_copy(block(slots.at[4], my_chip), got_ref.at[fifth],
                                      local_sem.at[5])
    pl.when(has_fifth)(own_fifth.start)
    attention(CHUNKS - 1)

    taken = []
    for s in range(4):
        copy = pltpu.make_async_copy(
            block(slots.at[s], my_chip), got_ref.at[jnp.maximum(spans[s], 0)], local_sem.at[s])
        pl.when(spans[s] >= 0)(copy.start)
        taken.append((spans[s] >= 0, copy))

    def landed(source):
        ref = got_ref.at[source]
        pltpu.make_async_copy(ref, ref, recv_r.at[source]).wait()

    def direct(zs, xs, core):
        cond = zs > z
        if xs == 1:
            cond = cond | ((zs == z) & (x == 0))
            cond = cond | (zs < z - 2) | ((zs == z - 2) & ((x == 1) | (core == 0)))
        else:
            cond = cond | ((zs == z - 1) & (x == 1) & (core == 0)) | (zs < z - 1)
        return cond

    chips = [(zs, xs) for zs in (3, 2, 1, 0) for xs in range(2)]
    for zs, xs in chips:
        source = 4 * zs + 2 * xs + c

        @pl.when(direct(zs, xs, c))
        def _(source=source):
            landed(source)
        go(direct(zs, xs, c), remote(got_ref.at[source], got_ref.at[source],
                                     send_x.at[2 * zs + xs], recv_r.at[source], sibling))
    landed(sibling)

    @pl.when((c == 1) & (me >= 6))
    def _():
        landed(jnp.maximum(me - 6, 0))
    for zs, xs in chips:
        source = 4 * zs + 2 * xs + 1 - c

        @pl.when(direct(zs, xs, 1 - c))
        def _(source=source):
            landed(source)

    pl.when(has_fifth)(own_fifth.wait)
    keep.wait()
    for cond, copy in taken:
        pl.when(cond)(copy.wait)
    for cond, copy in started:
        pl.when(cond)(copy.wait_send)


def unpack_kernel(got_ref, att_in, att_out, key_out, value_out):
    core = lax.axis_index("prefill") % 2
    cw = key_out.shape[1]
    r = lax.broadcasted_iota(jnp.int32, (128, 256), 0)
    t = lax.broadcasted_iota(jnp.int32, (128, 256), 1)
    moves = jnp.where(t == ((r & 15) << 4) + core * 8 + (r >> 4), 1.0, 0.0).astype(jnp.bfloat16)
    for out, base in ((key_out, 0), (value_out, cw)):
        for n in range(cw // 512):
            out[:, n * 512:(n + 1) * 512] = jnp.dot(
                moves, got_ref[:, base + n * 512:base + (n + 1) * 512],
                preferred_element_type=jnp.float32,
            ).astype(jnp.bfloat16)
    att_out[...] = att_in[...]


def planned(queries, keys, values, span_prompt, tails, owners):
    rows, width = queries.shape
    vmem = pl.BlockSpec(memory_space=pltpu.VMEM)
    smem = pl.BlockSpec(memory_space=pltpu.SMEM)
    dma = pltpu.SemaphoreType.DMA
    attended, got = pl.pallas_call(
        exchange_kernel,
        out_shape=(
            jax.ShapeDtypeStruct((rows, width), jnp.bfloat16),
            jax.ShapeDtypeStruct((16, 16, 2 * width), jnp.bfloat16),
        ),
        in_specs=[smem] * 3 + [vmem] * 3,
        out_specs=(vmem, pl.BlockSpec(memory_space=pl.ANY)),
        scratch_shapes=[
            pltpu.VMEM((rows, 2 * width), jnp.bfloat16),
            pltpu.VMEM((SLOTS, rows, 2 * width), jnp.bfloat16),
            dma((SLOTS, CHUNKS)),
            dma((3, CHUNKS)),
            dma((5, CHUNKS)),
            dma((16,)),
            dma((8,)),
            dma((5,)),
            dma((6,)),
            dma((8,)),
            dma((6,)),
        ],
        compiler_params=pltpu.CompilerParams(
            collective_id=0, has_side_effects=True, vmem_limit_bytes=52 * 2**20
        ),
        cost_estimate=pl.CostEstimate(
            flops=24 * rows * rows * width, bytes_accessed=32 * rows * width,
            transcendentals=MAXC * HEADS * rows * rows,
        ),
    )(span_prompt, tails, owners, queries, keys, values)
    cw = width // CHUNKS
    return pl.pallas_call(
        unpack_kernel,
        grid=(CHUNKS,),
        out_shape=(jax.ShapeDtypeStruct((rows, width), jnp.bfloat16),) * 3,
        in_specs=[
            pl.BlockSpec((256, 2 * cw), lambda n: (0, n)),
            pl.BlockSpec((rows, cw), lambda n: (0, n)),
        ],
        out_specs=(pl.BlockSpec((rows, cw), lambda n: (0, n)),) * 3,
        compiler_params=pltpu.CompilerParams(vmem_limit_bytes=32 * 2**20),
    )(got.reshape(256, 2 * width), attended)


def solution(mesh):
    placed = (
        P(("groups", "prefill"), None),
        P(("groups", "prefill"), None),
        P(("groups", "prefill"), None),
        P("groups"),
        P("groups"),
        P("groups"),
    )
    return jax.shard_map(
        planned if mesh.shape["prefill"] == 16 else local,
        mesh=mesh,
        in_specs=placed,
        out_specs=(
            P(("groups", "prefill"), None),
            P(("groups", "prefill"), None),
            P(("groups", "prefill"), None),
        ),
        check_vma=False,
    )
```

```python
import functools
import math
import jax
import jax.numpy as jnp
from jax import lax
from jax.experimental import pallas as pl
from jax.experimental.pallas import tpu as pltpu
from jax.sharding import PartitionSpec as P

HEADS = 64
MAXC = 6
CHUNKS = 8
SLOTS = 5
TOGETHER = 4
AHEAD = 4
MESH = pl.DeviceIdType.MESH


def from_behind(array, axis, by):
    devices = lax.axis_size(axis)
    pairs = [(i, i + by) for i in range(devices) if 0 <= i + by < devices]
    return lax.ppermute(array, axis, pairs)


def pick_entry(table, where_at):
    index = jnp.arange(table.shape[0], dtype=jnp.int32)
    return jnp.sum(jnp.where(index == where_at, table, 0))


def local(queries, keys, values, span_prompt, tails, owners):
    rows, width = queries.shape
    depth = width // HEADS
    count_dev = lax.axis_size("prefill")
    me_index = lax.axis_index("prefill")
    span_index = jnp.arange(span_prompt.shape[0], dtype=jnp.int32)
    prompt_id = pick_entry(span_prompt, me_index)
    mine = span_prompt == prompt_id
    order = jnp.sum(mine & (span_index < me_index))
    count = jnp.sum(mine)
    length = (count - 1) * rows + pick_entry(tails, prompt_id)
    owner = pick_entry(owners, prompt_id)
    local_rows = jnp.arange(rows, dtype=jnp.int32)
    query_pos = order * rows + local_rows
    used = query_pos < length
    blocks = [(keys, values)]
    carried = (keys, values)
    for step in range(1, MAXC):
        carried = from_behind((carried[0], carried[1]), "prefill", 1)
        blocks.append(carried)
    scale = 1.0 / depth**0.5
    query_heads = queries.reshape(rows, HEADS, depth)
    own_allowed = (local_rows[None, :] <= local_rows[:, None]) & (
        (order * rows + local_rows)[None, :] < length
    )
    scores = []
    allowed_list = []
    for step in range(MAXC):
        key_heads = blocks[step][0].reshape(rows, HEADS, depth)
        score = (
            jnp.einsum("qhd,khd->hqk", query_heads, key_heads, preferred_element_type=jnp.float32)
            * scale
        )
        if step == 0:
            allowed = own_allowed[None]
        else:
            allowed = jnp.broadcast_to(step <= order, (1, 1, 1))
        scores.append(score)
        allowed_list.append(allowed)
    top = jnp.full((HEADS, rows, 1), -jnp.inf, jnp.float32)
    for step in range(MAXC):
        masked = jnp.where(allowed_list[step], scores[step], -jnp.inf)
        top = jnp.maximum(top, jnp.max(masked, axis=-1, keepdims=True))
    total = jnp.zeros((HEADS, rows), jnp.float32)
    mixed = jnp.zeros((rows, HEADS, depth), jnp.float32)
    for step in range(MAXC):
        weight = jnp.where(allowed_list[step], jnp.exp(scores[step] - top), jnp.float32(0.0))
        total = total + jnp.sum(weight, axis=-1)
        value_heads = blocks[step][1].reshape(rows, HEADS, depth)
        mixed = mixed + jnp.einsum(
            "hqk,khd->qhd",
            weight.astype(jnp.bfloat16),
            value_heads,
            preferred_element_type=jnp.float32,
        )
    mixed = mixed / jnp.transpose(total)[:, :, None]
    mixed = jnp.where(used[:, None, None], mixed, jnp.float32(0.0))
    attended = mixed.reshape(rows, width).astype(jnp.bfloat16)
    masked_keys = jnp.where(used[:, None], keys, jnp.zeros_like(keys))
    masked_values = jnp.where(used[:, None], values, jnp.zeros_like(values))
    rolled_keys = jnp.roll(masked_keys.reshape(rows // count_dev, count_dev, width), owner, axis=1)
    rolled_values = jnp.roll(
        masked_values.reshape(rows // count_dev, count_dev, width), owner, axis=1
    )
    got_keys, got_values = (
        lax.all_to_all(rolled_keys, "prefill", split_axis=1, concat_axis=1, tiled=True),
        lax.all_to_all(rolled_values, "prefill", split_axis=1, concat_axis=1, tiled=True),
    )
    return (attended, got_keys.reshape(rows, width), got_values.reshape(rows, width))


def exchange_kernel(
    sp, tails, owners, q_ref, k_ref, v_ref, att_ref, got_ref,
    packed, slots, recv, send_a, send_b, recv_r, send_r, send_f, send_g, send_h, send_x, local_sem,
):
    rows, width = q_ref.shape
    depth = width // HEADS
    cw = width // CHUNKS
    me = lax.axis_index("prefill")
    z, x, c = me // 4, (me // 2) % 2, me % 2
    sibling = me + 1 - 2 * c
    others = [lax.rem(me + k, 16) for k in range(1, 16)]

    prompt = sp[me]
    order = jnp.int32(0)
    count = jnp.int32(0)
    for j in range(16):
        same = jnp.where(sp[j] == prompt, 1, 0)
        count = count + same
        order = order + jnp.where(j < me, same, 0)
    used_rows = (count - 1 - order) * rows + tails[prompt]
    owner = owners[prompt]
    spans = [
        4 * z - 4 * (1 - x),
        4 * z - 4 * (1 - x) + 1,
        4 * z - 2,
        4 * z - 1,
        jnp.where(c == 1, me - 1, me - 5),
    ]
    flags = [
        jnp.where(s >= 0, jnp.where(sp[jnp.maximum(s, 0)] == prompt, 1, 0), 0) for s in spans
    ]

    def clear(slot):
        @pl.loop(0, 2 * width // 512)
        def _(n):
            slots[slot, :, pl.ds(pl.multiple_of(n * 512, 512), 512)] = jnp.zeros(
                (rows, 512), jnp.bfloat16
            )

    for s in range(SLOTS):
        pl.when(spans[s] < 0)(functools.partial(clear, s))

    barrier = pltpu.get_barrier_semaphore()
    for other in others:
        pl.semaphore_signal(barrier, inc=1, device_id={"prefill": other}, device_id_type=MESH)
    pl.semaphore_wait(barrier, 15)

    def remote(src, dst, ssem, rsem, to):
        return pltpu.make_async_remote_copy(
            src_ref=src, dst_ref=dst, send_sem=ssem, recv_sem=rsem,
            device_id={"prefill": to}, device_id_type=MESH,
        )

    started = []

    def go(cond, copy):
        pl.when(cond)(copy.start)
        started.append((cond, copy))

    def cols(ch):
        return pl.ds(ch * 2 * cw, 2 * cw)

    zslot = 2 * x + c

    r = lax.broadcasted_iota(jnp.int32, (rows, rows), 0)
    t = lax.broadcasted_iota(jnp.int32, (rows, rows), 1)
    wanted = (((r >> 3) - owner) & 15) + ((r & 7) << 4)
    moves = jnp.where((t == wanted) & (t < used_rows), 1.0, 0.0).astype(jnp.bfloat16)
    for ch in range(CHUNKS):
        for part, ref in ((0, k_ref), (1, v_ref)):
            @pl.loop(0, cw // 256)
            def _(n, ch=ch, part=part, ref=ref):
                at = pl.multiple_of(n * 256, 256)
                block = ref[:, pl.ds(ch * cw + at, 256)]
                packed[:, pl.ds((2 * ch + part) * cw + at, 256)] = jnp.dot(
                    moves, block, preferred_element_type=jnp.float32
                ).astype(jnp.bfloat16)

        own = packed.at[:, cols(ch)]
        go(z < 3, remote(own, slots.at[zslot, :, cols(ch)], send_a.at[0, ch],
                         recv.at[zslot, ch], lax.rem(me + 4, 16)))
        go(x == 0, remote(own, slots.at[c, :, cols(ch)], send_a.at[1, ch],
                          recv.at[c, ch], lax.rem(me + 2, 16)))
        go(c == 0, remote(own, slots.at[4, :, cols(ch)], send_a.at[2, ch],
                          recv.at[4, ch], sibling))

    def block(ref, chip):
        return ref.at[pl.ds(pl.multiple_of(chip * 16, 16), 16), :]

    def piece(slot, chip, ch):
        return slots.at[slot, pl.ds(pl.multiple_of(chip * 16, 16), 16), cols(ch)]

    my_chip = me // 2
    keep = pltpu.make_async_copy(block(packed, my_chip), got_ref.at[me], local_sem.at[4])
    keep.start()
    go(me >= 0, remote(block(packed, my_chip), got_ref.at[me], send_r.at[7], recv_r.at[me], sibling))
    go(x == 1, remote(block(packed, lax.rem(my_chip + 7, 8)), got_ref.at[me], send_r.at[6],
                      recv_r.at[me], lax.rem(me + 14, 16)))
    for zp in (2, 1, 0):
        for xp in range(2):
            go((zp < z) & ((x == 1) | (xp == 0)), remote(
                block(packed, 2 * zp + xp), got_ref.at[me], send_r.at[2 * zp + xp],
                recv_r.at[me], 4 * zp + 2 * xp + c))

    def arrived(slot, ch):
        ref = slots.at[slot, :, cols(ch)]
        pltpu.make_async_copy(ref, ref, recv.at[slot, ch]).wait()

    def relay(ch):
        @pl.when(z >= 1)
        def _():
            arrived(zslot, ch)
        here = slots.at[zslot, :, cols(ch)]
        go((z >= 1) & (x == 1), remote(here, slots.at[2 + c, :, cols(ch)], send_b.at[0, ch],
                                       recv.at[2 + c, ch], lax.rem(me + 14, 16)))
        go((z >= 1) & (x == 0) & (c == 1), remote(here, slots.at[4, :, cols(ch)], send_b.at[1, ch],
                                                  recv.at[4, ch], lax.rem(me + 1, 16)))
        go(z >= 1, remote(here, slots.at[zslot, :, cols(ch)], send_b.at[2, ch],
                          recv.at[zslot, ch], sibling))
        origin = lax.rem(me + 12, 16)
        into = got_ref.at[origin, :, cols(ch)]
        go((z >= 1) & (x == 0) & (c == 0), remote(
            piece(zslot, lax.rem(my_chip + 1, 8), ch), into,
            send_f.at[0, ch], recv_r.at[origin], lax.rem(me + 2, 16)))
        for zp in (3, 2):
            for xp in range(2):
                cond = (z >= 1) & (zp > z) & (c == 0)
                if zp == 3 and xp == 1:
                    cond = cond & ((z < 2) | (x == 1))
                go(cond, remote(
                    piece(zslot, 2 * zp + xp, ch), into,
                    send_f.at[1 + 2 * (zp - 2) + xp, ch], recv_r.at[origin],
                    4 * zp + 2 * xp + c))
        second = 2 * (1 - x) + c
        has = (x == 1) | (z >= 1)

        @pl.when(has)
        def _():
            arrived(second, ch)
        there = slots.at[second, :, cols(ch)]
        if ch < CHUNKS * 3 // 4:
            go((x == 0) & (z >= 1) & (z < 3) & (c == 1),
               remote(there, slots.at[4, :, cols(ch)], send_b.at[3, ch], recv.at[4, ch],
                      lax.rem(me + 3, 16)))
        else:
            go((x == 1) & (z >= 1) & (z < 3) & (c == 1),
               remote(here, slots.at[4, :, cols(ch)], send_b.at[3, ch], recv.at[4, ch],
                      lax.rem(me + 1, 16)))
        go(has, remote(there, slots.at[second, :, cols(ch)], send_b.at[4, ch],
                       recv.at[second, ch], sibling))
        go((z == 1) & (x == 1) & (c == 0), remote(
            piece(second, 7, ch), got_ref.at[lax.rem(me + 14, 16), :, cols(ch)],
            send_h.at[3, ch], recv_r.at[lax.rem(me + 14, 16)], 14))
        origin = lax.rem(me + 14, 16)
        for zp in (2, 1, 0):
            go((x == 1) & (zp < z), remote(
                piece(second, 2 * zp + 1, ch), got_ref.at[origin, :, cols(ch)],
                send_h.at[zp, ch], recv_r.at[origin], 4 * zp + 2 + c))

    scale = math.log2(math.e) / depth**0.5
    causal = (t <= r) & (t < used_rows)
    keep_row = lax.broadcasted_iota(jnp.int32, (rows, depth), 0) < used_rows
    masks = [jnp.full((rows, rows), f, jnp.int32) > 0 for f in flags]

    fifth = jnp.maximum(spans[4], 0)
    has_fifth = (c == 0) & (spans[4] >= 0)

    def attention(ch):
        @pl.when(z >= 1)
        def _():
            arrived(2 * x + (1 - c), ch)

        @pl.when((x == 1) | (z >= 1))
        def _():
            arrived(2 * (1 - x) + (1 - c), ch)

        @pl.when(spans[4] >= 0)
        def _():
            arrived(4, ch)
        into = got_ref.at[fifth, :, cols(ch)]
        for zp in (3, 2):
            for xp in range(2):
                go(has_fifth & (zp > z), remote(
                    piece(4, 2 * zp + xp, ch), into,
                    send_g.at[2 * (zp - 2) + xp, ch], recv_r.at[fifth],
                    4 * zp + 2 * xp + 1 - c))
        go(has_fifth & (x == 0), remote(
            piece(4, lax.rem(my_chip + 1, 8), ch), into,
            send_g.at[4, ch], recv_r.at[fifth], lax.rem(me + 3, 16)))
        go(has_fifth, remote(piece(4, my_chip, ch), into, send_g.at[5, ch],
                             recv_r.at[fifth], sibling))

        def head(at):
            mine = pl.ds(ch * cw + at, depth)
            kcols = pl.ds(2 * ch * cw + at, depth)
            vcols = pl.ds((2 * ch + 1) * cw + at, depth)
            q = q_ref[:, mine]
            dims = (((1,), (1,)), ((), ()))
            scores = [
                jnp.where(causal, lax.dot_general(
                    q, k_ref[:, mine], dims, preferred_element_type=jnp.float32), -jnp.inf)
            ]
            for s in range(SLOTS):
                score = lax.dot_general(
                    q, slots[s, :, kcols], dims, preferred_element_type=jnp.float32)
                scores.append(jnp.where(masks[s], score, -jnp.inf))
            top = functools.reduce(jnp.maximum, scores)
            top = jnp.max(top, axis=1, keepdims=True)
            weights = [jnp.exp2((s - top) * scale) for s in scores]
            total = jnp.sum(functools.reduce(jnp.add, weights), axis=1, keepdims=True)
            mixed = jnp.dot(weights[0].astype(jnp.bfloat16), v_ref[:, mine],
                            preferred_element_type=jnp.float32)
            for s in range(SLOTS):
                mixed = mixed + jnp.dot(weights[s + 1].astype(jnp.bfloat16), slots[s, :, vcols],
                                        preferred_element_type=jnp.float32)
            mixed = jnp.where(keep_row, mixed / total, 0.0)
            att_ref[:, mine] = mixed.astype(jnp.bfloat16)

        @pl.loop(0, HEADS // CHUNKS // TOGETHER)
        def _(n):
            for m in range(TOGETHER):
                head(pl.multiple_of((n * TOGETHER + m) * depth, depth))

    for ch in range(CHUNKS + AHEAD):
        if ch < CHUNKS:
            relay(ch)
        if ch >= AHEAD:
            attention(ch - AHEAD)

    own_fifth = pltpu.make_async_copy(block(slots.at[4], my_chip), got_ref.at[fifth],
                                      local_sem.at[5])
    pl.when(has_fifth)(own_fifth.start)
    taken = []
    for s in range(4):
        copy = pltpu.make_async_copy(
            block(slots.at[s], my_chip), got_ref.at[jnp.maximum(spans[s], 0)], local_sem.at[s])
        pl.when(spans[s] >= 0)(copy.start)
        taken.append((spans[s] >= 0, copy))

    def landed(source):
        ref = got_ref.at[source]
        pltpu.make_async_copy(ref, ref, recv_r.at[source]).wait()

    def direct(zs, xs, core):
        cond = zs > z
        if xs == 1:
            cond = cond | ((zs == z) & (x == 0))
            cond = cond | (zs < z - 2) | ((zs == z - 2) & ((x == 1) | (core == 0)))
        else:
            cond = cond | ((zs == z - 1) & (x == 1) & (core == 0)) | (zs < z - 1)
        return cond

    chips = [(zs, xs) for zs in (3, 2, 1, 0) for xs in range(2)]
    for zs, xs in chips:
        source = 4 * zs + 2 * xs + c

        @pl.when(direct(zs, xs, c))
        def _(source=source):
            landed(source)
        go(direct(zs, xs, c), remote(got_ref.at[source], got_ref.at[source],
                                     send_x.at[2 * zs + xs], recv_r.at[source], sibling))
    landed(sibling)

    @pl.when((c == 1) & (me >= 6))
    def _():
        landed(jnp.maximum(me - 6, 0))
    for zs, xs in chips:
        source = 4 * zs + 2 * xs + 1 - c

        @pl.when(direct(zs, xs, 1 - c))
        def _(source=source):
            landed(source)

    pl.when(has_fifth)(own_fifth.wait)
    keep.wait()
    for cond, copy in taken:
        pl.when(cond)(copy.wait)
    for cond, copy in started:
        pl.when(cond)(copy.wait_send)


def unpack_kernel(got_ref, att_in, att_out, key_out, value_out):
    core = lax.axis_index("prefill") % 2
    cw = key_out.shape[1]
    r = lax.broadcasted_iota(jnp.int32, (128, 256), 0)
    t = lax.broadcasted_iota(jnp.int32, (128, 256), 1)
    moves = jnp.where(t == ((r & 15) << 4) + core * 8 + (r >> 4), 1.0, 0.0).astype(jnp.bfloat16)
    for out, base in ((key_out, 0), (value_out, cw)):
        for n in range(cw // 512):
            out[:, n * 512:(n + 1) * 512] = jnp.dot(
                moves, got_ref[:, base + n * 512:base + (n + 1) * 512],
                preferred_element_type=jnp.float32,
            ).astype(jnp.bfloat16)
    att_out[...] = att_in[...]


def planned(queries, keys, values, span_prompt, tails, owners):
    rows, width = queries.shape
    vmem = pl.BlockSpec(memory_space=pltpu.VMEM)
    smem = pl.BlockSpec(memory_space=pltpu.SMEM)
    dma = pltpu.SemaphoreType.DMA
    attended, got = pl.pallas_call(
        exchange_kernel,
        out_shape=(
            jax.ShapeDtypeStruct((rows, width), jnp.bfloat16),
            jax.ShapeDtypeStruct((16, 16, 2 * width), jnp.bfloat16),
        ),
        in_specs=[smem] * 3 + [vmem] * 3,
        out_specs=(vmem, pl.BlockSpec(memory_space=pl.ANY)),
        scratch_shapes=[
            pltpu.VMEM((rows, 2 * width), jnp.bfloat16),
            pltpu.VMEM((SLOTS, rows, 2 * width), jnp.bfloat16),
            dma((SLOTS, CHUNKS)),
            dma((3, CHUNKS)),
            dma((5, CHUNKS)),
            dma((16,)),
            dma((8,)),
            dma((5, CHUNKS)),
            dma((6, CHUNKS)),
            dma((4, CHUNKS)),
            dma((8,)),
            dma((6,)),
        ],
        compiler_params=pltpu.CompilerParams(
            collective_id=0, has_side_effects=True, vmem_limit_bytes=52 * 2**20
        ),
        cost_estimate=pl.CostEstimate(
            flops=24 * rows * rows * width, bytes_accessed=32 * rows * width,
            transcendentals=MAXC * HEADS * rows * rows,
        ),
    )(span_prompt, tails, owners, queries, keys, values)
    cw = width // CHUNKS
    return pl.pallas_call(
        unpack_kernel,
        grid=(CHUNKS,),
        out_shape=(jax.ShapeDtypeStruct((rows, width), jnp.bfloat16),) * 3,
        in_specs=[
            pl.BlockSpec((256, 2 * cw), lambda n: (0, n)),
            pl.BlockSpec((rows, cw), lambda n: (0, n)),
        ],
        out_specs=(pl.BlockSpec((rows, cw), lambda n: (0, n)),) * 3,
        compiler_params=pltpu.CompilerParams(vmem_limit_bytes=32 * 2**20),
    )(got.reshape(256, 2 * width), attended)


def solution(mesh):
    placed = (
        P(("groups", "prefill"), None),
        P(("groups", "prefill"), None),
        P(("groups", "prefill"), None),
        P("groups"),
        P("groups"),
        P("groups"),
    )
    return jax.shard_map(
        planned if mesh.shape["prefill"] == 16 else local,
        mesh=mesh,
        in_specs=placed,
        out_specs=(
            P(("groups", "prefill"), None),
            P(("groups", "prefill"), None),
            P(("groups", "prefill"), None),
        ),
        check_vma=False,
    )
```
